32 devices in a mesh: bricks: 8 (over z, y), rep: 4 (over x, core).
Axes of the slice: x: 2, y: 2, z: 4, core: 2. Of those that a mesh axis runs over, the one named last changes fastest.
Arguments:
- features: bfloat16 [4, 176, 8, 8, 8, 128], P('rep', 'bricks'), may hold values from -6 to 6
- cotangent: bfloat16 [4, 176, 8, 8, 8, 128], P('rep', 'bricks'), may hold values from -6 to 6
- occupancy: int32 [4, 176, 512], P('rep', 'bricks'), may hold values 0 or 1
- fine_parent: int32 [4, 176], P('rep', 'bricks'), may hold values from 0 to 23, as said below
- fine_octant: int32 [4, 176], P('rep', 'bricks'), may hold values from 0 to 7
- w_down: bfloat16 [3, 3, 3, 128, 128], replicated, may hold values from -0.109375 to 0.109375
- w_up: bfloat16 [3, 3, 3, 128, 128], replicated, may hold values from -0.1875 to 0.1875
- bias: float32 [128], replicated, may hold values from -3 to 3
Outputs:
- grad_features: bfloat16 [4, 176, 8, 8, 8, 128], P('rep', 'bricks')
- grad_down: float32 [27, 16384], P(None, 'bricks')
- grad_up: float32 [27, 16384], P(None, 'bricks')
The draws below stay inside these ranges and needn't reach their ends.
Inputs may be any that keep to these rules, and one draw needn't show every extreme that they name: `fine_parent`: coarse brick q of a replica is owned by index q // 3 of bricks; no two fine bricks of a replica share parent and octant; the fine bricks held by index s of bricks have parents owned by indices s, s + 1, ..., s + 4 - 1 modulo the size of bricks, with 4 = 4, at most 6 of them by one owner (6 = 22 / 4 rounded up, with 4 = 4), and that most is reached on every device; each device owns the parents of exactly 22 fine bricks.
All inputs are finite; a program needn't handle non-finite values. No bound on the sum of `occupancy` on one device may be relied on, other than what follows from the above.
Results may differ from the reference program's by a relative error of at most 0.0051.
Values may be sent and summed in bfloat16 or wider, within the bound.
A program may use at most 64 MiB of HBM per device.

```python
import jax
import jax.numpy as jnp
from jax import lax

C = 128
FB_DEV = 22
CAP = 6
CB_DEV = 3
FINE = 176
COARSE = 24
REPS = 4
N_BRICKS = 8


def routing(base_key):

    def single(replica_key):
        first_key, second_key = jax.random.split(replica_key)
        shuffled = jax.vmap(lambda sub_key: jax.random.permutation(sub_key, FB_DEV))(jax.random.split(first_key, N_BRICKS)).astype(jnp.int32)
        source = jnp.arange(N_BRICKS, dtype=jnp.int32)[:, None]
        target = (source + shuffled // CAP) % N_BRICKS
        labels = jax.vmap(lambda sub_key: jax.random.permutation(sub_key, 8 * CB_DEV))(jax.random.split(second_key, N_BRICKS)).astype(jnp.int32)
        placed = labels[target, shuffled]
        return ((target * CB_DEV + placed // 8).reshape(-1), (placed % 8).reshape(-1))
    return jax.vmap(single)(jax.random.split(jax.random.fold_in(base_key, 17), REPS))


def draw_fine_parent(key, part):
    return routing(key)[0].astype(jnp.int32)


def draw_fine_octant(key, part):
    return routing(key)[1].astype(jnp.int32)


def plant(values, rng, low, top_value):
    extent = values.shape
    spot = [jax.random.randint(jax.random.fold_in(rng, axis), (), 0, extent[axis]) for axis in range(len(extent))]
    values = values.at[tuple(spot)].set(low)
    longest = extent.index(max(extent))
    spot[longest] = (spot[longest] + 1) % extent[longest]
    return values.at[tuple(spot)].set(top_value)


def shard_levels(stream_key, dims, cuts, smallest, largest):
    def one(position, shards_of):
        steps = jax.random.uniform(jax.random.fold_in(jax.random.fold_in(stream_key, 6), position), (shards_of,), jnp.float32, smallest / len(cuts), largest / len(cuts))
        return jnp.repeat(jnp.exp(steps), dims[position] // shards_of).reshape((-1,) + (1,) * (len(dims) - position - 1))

    gain = one(*cuts[0])
    for cut in cuts[1:]:
        gain = gain * one(*cut)
    return gain


def normal_values(key, shape, deviation, limit, shards=(), kind=jnp.bfloat16):
    loudness = shard_levels(key, shape, shards, -0.22, 0.18) if shards else 1.0
    values = jax.random.normal(key, shape, jnp.float32) * deviation * loudness
    return jnp.minimum(jnp.maximum(values, -limit), limit).astype(kind)


def setup_inputs(seed: int = 0) -> dict:
    seeds = jax.random.split(jax.random.key(seed), 9)
    features = normal_values(seeds[0], (REPS, FINE, 8, 8, 8, C), 1.0, 6.0, ((0, 4), (1, 8)))
    cotangent = normal_values(seeds[1], (REPS, FINE, 8, 8, 8, C), 1.0, 6.0, ((0, 4), (1, 8)))
    occupancy = plant((jax.random.randint(seeds[2], (REPS, FINE, 512), 0, 4) < 3).astype(jnp.int32), jax.random.fold_in(seeds[2], 1), 0, 1)
    fine_parent = draw_fine_parent(jax.random.fold_in(seeds[8], 71), 0)
    fine_octant = draw_fine_octant(jax.random.fold_in(seeds[8], 71), 0)
    w_down = normal_values(seeds[5], (3, 3, 3, C, C), (27 * C) ** -0.5, 0.109375)
    w_up = normal_values(seeds[6], (3, 3, 3, C, C), (8 * C) ** -0.5, 0.1875)
    bias = normal_values(seeds[7], (C,), 0.7, 3.0, (), jnp.float32)
    return {"features": features, "cotangent": cotangent, "occupancy": occupancy, "fine_parent": fine_parent, "fine_octant": fine_octant, "w_down": w_down, "w_up": w_up, "bias": bias}


NUMBERS = ('NDHWC', 'DHWIO', 'NDHWC')

def pad_brick(values):
    return jnp.pad(values, ((0, 0), (1, 2), (1, 2), (1, 2), (0, 0)))

def down_conv(padded, weight):
    return lax.conv_general_dilated(padded, weight, (2, 2, 2), 'VALID', dimension_numbers=NUMBERS, preferred_element_type=jnp.float32)

def adjoint_conv(window, weight):
    turned = jnp.swapaxes(weight[::-1, ::-1, ::-1], 3, 4)
    return lax.conv_general_dilated(window, turned, (1, 1, 1), ((2, 2), (2, 2), (2, 2)), lhs_dilation=(2, 2, 2), dimension_numbers=NUMBERS, preferred_element_type=jnp.float32)

def weight_grad(padded, window):
    result = lax.conv_general_dilated(padded, window, (1, 1, 1), 'VALID', rhs_dilation=(2, 2, 2), dimension_numbers=('CDHWN', 'IDHWO', 'NDHWC'), preferred_element_type=jnp.float32)
    return jnp.transpose(result, (1, 2, 3, 0, 4)).reshape(27, result.shape[0], result.shape[4])

def corner_offsets(corner):
    return (4 * (corner // 4), 4 * (corner // 2 % 2), 4 * (corner % 2))

def place_windows(windows, parent, octant):
    summed_field = jnp.zeros((COARSE, 9, 9, 9, windows.shape[-1]), jnp.float32)
    for corner in range(8):
        start_x, start_y, start_z = corner_offsets(corner)
        chosen = jnp.where((octant == corner)[:, None, None, None, None], windows.astype(jnp.float32), 0.0)
        summed = jax.ops.segment_sum(chosen, parent, num_segments=COARSE)
        summed_field = summed_field.at[:, start_x:start_x + 5, start_y:start_y + 5, start_z:start_z + 5].add(summed)
    return summed_field[:, :8, :8, :8]

def reference(features, cotangent, occupancy, fine_parent, fine_octant, w_down, w_up, bias):
    channels = features.shape[-1]
    swapped_up = jnp.swapaxes(w_up, 3, 4)
    running = (jnp.zeros((27, channels, channels), jnp.float32), jnp.zeros((27, channels, channels), jnp.float32))
    outputs = []
    for replica in range(REPS):
        occupied = occupancy[replica].reshape(FINE, 8, 8, 8, 1).astype(features.dtype)
        masked_x = (features[replica] * occupied).reshape(N_BRICKS, FB_DEV, 8, 8, 8, channels)
        masked_g = (cotangent[replica] * occupied).reshape(N_BRICKS, FB_DEV, 8, 8, 8, channels)

        def partials(paired):
            first = down_conv(pad_brick(paired[0]), w_down).astype(jnp.bfloat16)
            second = down_conv(pad_brick(paired[1]), swapped_up).astype(jnp.bfloat16)
            return (first, second)
        down_win, up_win = lax.map(partials, (masked_x, masked_g))
        down_win = down_win.reshape(FINE, 5, 5, 5, channels)
        up_win = up_win.reshape(FINE, 5, 5, 5, channels)
        parent = fine_parent[replica]
        octant = fine_octant[replica]
        pre = place_windows(down_win, parent, octant) + bias
        hidden = jax.nn.silu(pre).astype(jnp.bfloat16)
        grad_hidden = place_windows(up_win, parent, octant)
        sigmoid_pre = jax.nn.sigmoid(pre)
        grad_pre = (grad_hidden * sigmoid_pre * (1.0 + pre * (1.0 - sigmoid_pre))).astype(jnp.bfloat16)
        hidden_pad = jnp.pad(hidden, ((0, 0), (0, 1), (0, 1), (0, 1), (0, 0)))
        grad_pad = jnp.pad(grad_pre, ((0, 0), (0, 1), (0, 1), (0, 1), (0, 0)))

        def cut(coarse_field, parent_row, corner):
            start_x, start_y, start_z = corner_offsets(corner.astype(jnp.int32))
            anchor = jnp.zeros((), jnp.int32)
            return lax.dynamic_slice(coarse_field[parent_row], (start_x, start_y, start_z, anchor), (5, 5, 5, channels))

        def block_step(totals, block_items):
            block_x, block_g, block_c, block_m, block_parent, block_octant = block_items
            hidden_win = jax.vmap(cut, (None, 0, 0))(hidden_pad, block_parent, block_octant)
            grad_win = jax.vmap(cut, (None, 0, 0))(grad_pad, block_parent, block_octant)
            padded_x = pad_brick(block_x)
            padded_g = pad_brick(block_g)
            returned = adjoint_conv(grad_win, w_down)[:, 1:9, 1:9, 1:9]
            result = (block_c.astype(jnp.float32) + block_m.astype(jnp.float32) * returned).astype(jnp.bfloat16)
            new_down = totals[0] + weight_grad(padded_x, grad_win)
            new_up = totals[1] + jnp.swapaxes(weight_grad(padded_g, hidden_win), 1, 2)
            return ((new_down, new_up), result)
        blocks = (masked_x, masked_g, cotangent[replica].reshape(N_BRICKS, FB_DEV, 8, 8, 8, channels), occupied.reshape(N_BRICKS, FB_DEV, 8, 8, 8, 1), parent.reshape(N_BRICKS, FB_DEV), octant.reshape(N_BRICKS, FB_DEV))
        running, result = lax.scan(block_step, running, blocks)
        outputs.append(result.reshape(FINE, 8, 8, 8, channels))
    grad_down = (running[0] / FINE).reshape(27, channels * channels)
    grad_up = (running[1] / FINE).reshape(27, channels * channels)
    return (jnp.stack(outputs), grad_down, grad_up)
```

```python
import functools

import jax
import jax.numpy as jnp
from jax import lax
from jax.experimental import pallas as pl
from jax.experimental.pallas import tpu as pltpu
from jax.sharding import PartitionSpec as P

OWNERS = 4


NUMBERS = ("NDHWC", "DHWIO", "NDHWC")


def as_sent(shard):
    return jax.tree.map(lambda a: a.astype(jnp.bfloat16) if a.dtype == jnp.float32 else a, shard)


def shifted(shard, axis, by):
    length = lax.axis_size(axis)
    return lax.ppermute(shard, axis, [(i, (i + by) % length) for i in range(length)])


def pad_brick(values):
    return jnp.pad(values, ((0, 0), (1, 2), (1, 2), (1, 2), (0, 0)))


def down_conv(padded, weight):
    return lax.conv_general_dilated(
        padded,
        weight,
        (2, 2, 2),
        "VALID",
        dimension_numbers=NUMBERS,
        preferred_element_type=jnp.float32,
    )


def adjoint_conv(window, weight):
    turned = jnp.swapaxes(weight[::-1, ::-1, ::-1], 3, 4)
    return lax.conv_general_dilated(
        window,
        turned,
        (1, 1, 1),
        ((2, 2), (2, 2), (2, 2)),
        lhs_dilation=(2, 2, 2),
        dimension_numbers=NUMBERS,
        preferred_element_type=jnp.float32,
    )


def weight_grad(padded, window):
    result = lax.conv_general_dilated(
        padded,
        window,
        (1, 1, 1),
        "VALID",
        rhs_dilation=(2, 2, 2),
        dimension_numbers=("CDHWN", "IDHWO", "NDHWC"),
        preferred_element_type=jnp.float32,
    )
    return jnp.transpose(result, (1, 2, 3, 0, 4)).reshape(27, result.shape[0], result.shape[4])


def corner_offsets(corner):
    return (4 * (corner // 4), 4 * (corner // 2 % 2), 4 * (corner % 2))


def spread(items, mover):
    owner_count = items[0].shape[0]
    moved = [tuple((item[0] for item in items))]
    for offset in range(1, owner_count):
        moved.append(mover(tuple((item[offset] for item in items)), offset))
    return tuple((jnp.stack([entry[number] for entry in moved]) for number in range(len(items))))


def reduce_kernel(
    peers, scale, src, out, got_a, kept, got_b, part, got_c, send_a, recv_a, send_b, recv_b, send_c, recv_c, send_d, recv_d
):
    rep = lax.axis_index("rep")
    me = lax.axis_index("bricks")
    low, high = rep % 2, rep // 2
    near = {"rep": high * 2 + 1 - low}
    far = {"rep": (1 - high) * 2 + low}

    def brick(step):
        return (me + step) % peers

    def remote(source, target, send, recv, device):
        return pltpu.make_async_remote_copy(
            src_ref=source,
            dst_ref=target,
            send_sem=send,
            recv_sem=recv,
            device_id=device,
            device_id_type=pl.DeviceIdType.MESH,
        )

    barrier = pltpu.get_barrier_semaphore()
    for device in [near, far] + [{"bricks": brick(step)} for step in range(1, peers)]:
        pl.semaphore_signal(barrier, inc=1, device_id=device, device_id_type=pl.DeviceIdType.MESH)
    pl.semaphore_wait(barrier, peers + 1)

    halves = [1 - high, high]
    copies_a = [
        remote(src.at[1 - low, half], got_a.at[half], send_a.at[number], recv_a.at[number], near)
        for number, half in enumerate(halves)
    ]
    for copy in copies_a:
        copy.start()

    def add_half(half):
        @pl.loop(0, peers)
        def _(b):
            total = src[low, half, b].astype(jnp.float32) + got_a[half, b].astype(jnp.float32)
            kept[half, b] = total.astype(jnp.bfloat16)

    copies_a[0].wait_recv()
    add_half(halves[0])
    order = list(range(1, peers)) + [0]
    copies_b = [
        remote(
            kept.at[halves[0], brick(step)],
            got_b.at[brick(step)],
            send_b.at[step],
            recv_b.at[step],
            far,
        )
        for step in range(peers)
    ]
    for step in order:
        copies_b[step].start()
    copies_a[1].wait_recv()
    add_half(halves[1])

    copies_c = []
    mine = None
    for step in order:
        copies_b[step].wait_recv()
        b = brick(step)
        total = kept[halves[1], b].astype(jnp.float32) + got_b[b].astype(jnp.float32)
        if step == 0:
            mine = total
        else:
            part[b] = total.astype(jnp.bfloat16)
            copy = remote(
                part.at[b],
                got_c.at[step - 1],
                send_c.at[step - 1],
                recv_c.at[step - 1],
                {"bricks": b},
            )
            copy.start()
            copies_c.append(copy)
    for number, copy in enumerate(copies_c):
        copy.wait_recv()
        mine = mine + got_c[number].astype(jnp.float32)
    out[low, high] = mine * scale

    own = out.at[low, high]
    other = out.at[low, 1 - high]
    copies_d = [
        remote(own, own, send_d.at[0], recv_d.at[0], far),
        remote(own, own, send_d.at[1], recv_d.at[1], near),
        remote(other, other, send_d.at[2], recv_d.at[2], near),
    ]
    copies_d[0].start()
    copies_d[1].start()
    copies_d[0].wait_recv()
    copies_d[2].start()
    copies_d[1].wait_recv()
    copies_d[2].wait_recv()
    for copy in copies_a + copies_b + copies_c + copies_d:
        copy.wait_send()


def reduce_terms(terms, peers, scale):
    channels = terms[0].shape[1]
    own_rows = channels // peers
    rows = len(terms) * 27 * own_rows
    quarter = -(-rows // 64) * 16
    blocks = [
        jnp.swapaxes(term.astype(jnp.bfloat16).reshape(27, peers, own_rows, channels), 0, 1)
        for term in terms
    ]
    src = jnp.concatenate(blocks, axis=1).reshape(peers, rows, channels)
    src = jnp.pad(src, ((0, 0), (0, 4 * quarter - rows), (0, 0)))
    src = jnp.swapaxes(src.reshape(peers, 4, quarter, channels), 0, 1)
    src = src.reshape(2, 2, peers, quarter, channels)
    dma = pltpu.SemaphoreType.DMA
    wire = jnp.bfloat16
    out = pl.pallas_call(
        functools.partial(reduce_kernel, peers, scale),
        out_shape=jax.ShapeDtypeStruct((2, 2, quarter, channels), jnp.float32),
        in_specs=[pl.BlockSpec(memory_space=pltpu.VMEM)],
        out_specs=pl.BlockSpec(memory_space=pltpu.VMEM),
        scratch_shapes=[
            pltpu.VMEM((2, peers, quarter, channels), wire),
            pltpu.VMEM((2, peers, quarter, channels), wire),
            pltpu.VMEM((peers, quarter, channels), wire),
            pltpu.VMEM((peers, quarter, channels), wire),
            pltpu.VMEM((peers - 1, quarter, channels), wire),
            dma((2,)),
            dma((2,)),
            dma((peers,)),
            dma((peers,)),
            dma((peers - 1,)),
            dma((peers - 1,)),
            dma((3,)),
            dma((3,)),
        ],
        compiler_params=pltpu.CompilerParams(
            collective_id=0, has_side_effects=True, vmem_limit_bytes=32 * 1024 * 1024
        ),
    )(src)
    out = out.reshape(4 * quarter, channels)[:rows].reshape(len(terms), 27, own_rows * channels)
    return tuple(out[number] for number in range(len(terms)))


def body(features, cotangent, occupancy, fine_parent, fine_octant, w_down, w_up, bias):
    peer_count = lax.axis_size("bricks")
    my_index = lax.axis_index("bricks")
    bricks_here = features.shape[1]
    channels = features.shape[-1]
    owner_count = OWNERS
    capacity = (bricks_here + owner_count - 1) // owner_count
    coarse_here = (bricks_here + 7) // 8
    slot_count = owner_count * capacity
    occupied = occupancy[0].reshape(bricks_here, 8, 8, 8, 1).astype(jnp.bfloat16)
    padded_x = pad_brick(features[0] * occupied)
    padded_g = pad_brick(cotangent[0] * occupied)
    parent = fine_parent[0]
    octant = fine_octant[0]
    owner_offset = (parent // coarse_here - my_index) % peer_count
    position = jnp.arange(bricks_here, dtype=jnp.int32)
    earlier = (owner_offset[:, None] == owner_offset[None, :]) & (
        position[None, :] < position[:, None]
    )
    slot_of = owner_offset * capacity + jnp.sum(earlier.astype(jnp.int32), axis=1)
    dispatch = (slot_of[None, :] == jnp.arange(slot_count, dtype=jnp.int32)[:, None]).astype(
        jnp.bfloat16
    )
    labels_fine = (1 + parent % coarse_here * 8 + octant).astype(jnp.bfloat16)
    slot_label = (
        jnp.dot(dispatch, labels_fine, preferred_element_type=jnp.float32)
        .astype(jnp.bfloat16)
        .reshape(owner_count, capacity)
    )

    def to_slots(window):
        sent = jnp.dot(
            dispatch, window.reshape(bricks_here, -1), preferred_element_type=jnp.float32
        )
        return sent.astype(jnp.bfloat16).reshape(owner_count, capacity, 5, 5, 5, channels)

    def from_slots(arrived):
        taken = jnp.dot(
            dispatch.T, arrived.reshape(slot_count, -1), preferred_element_type=jnp.float32
        )
        return taken.astype(jnp.bfloat16).reshape(bricks_here, 5, 5, 5, channels)

    def gather_coarse(assignment, arrived):
        windows = jnp.dot(
            assignment, arrived.reshape(slot_count, -1), preferred_element_type=jnp.float32
        )
        windows = windows.reshape(coarse_here, 8, 5, 5, 5, channels)
        summed_field = jnp.zeros((coarse_here, 9, 9, 9, channels), jnp.float32)
        for corner in range(8):
            start_x, start_y, start_z = corner_offsets(corner)
            summed_field = summed_field.at[
                :, start_x : start_x + 5, start_y : start_y + 5, start_z : start_z + 5
            ].add(windows[:, corner])
        return summed_field[:, :8, :8, :8]

    def coarse_windows(assignment, coarse_field):
        padded = jnp.pad(coarse_field, ((0, 0), (0, 1), (0, 1), (0, 1), (0, 0)))
        pieces = []
        for corner in range(8):
            start_x, start_y, start_z = corner_offsets(corner)
            pieces.append(
                padded[:, start_x : start_x + 5, start_y : start_y + 5, start_z : start_z + 5]
            )
        stacked = jnp.stack(pieces, axis=1).reshape(coarse_here * 8, -1)
        sent = jnp.dot(assignment.T, stacked, preferred_element_type=jnp.float32)
        return sent.astype(jnp.bfloat16).reshape(owner_count, capacity, 5, 5, 5, channels)

    swapped_up = jnp.swapaxes(w_up, 3, 4)
    down_win = down_conv(padded_x, w_down).astype(jnp.bfloat16)
    arrived_down, arrived_labels = spread(
        (to_slots(down_win), slot_label),
        lambda pieces, offset: jax.tree.map(
            lambda part, own: part.astype(own.dtype),
            shifted(as_sent(pieces), "bricks", offset),
            pieces,
        ),
    )
    flat_labels = arrived_labels.reshape(slot_count).astype(jnp.float32)
    targets = (1 + jnp.arange(coarse_here * 8, dtype=jnp.int32)).astype(jnp.float32)
    assignment = (flat_labels[None, :] == targets[:, None]).astype(jnp.bfloat16)
    pre = gather_coarse(assignment, arrived_down) + bias
    sigmoid_pre = jax.nn.sigmoid(pre)
    hidden = jax.nn.silu(pre).astype(jnp.bfloat16)
    slope = sigmoid_pre * (1.0 + pre * (1.0 - sigmoid_pre))
    back_hidden = spread(
        (coarse_windows(assignment, hidden),),
        lambda pieces, offset: jax.tree.map(
            lambda part, own: part.astype(own.dtype),
            shifted(as_sent(pieces), "bricks", peer_count - offset),
            pieces,
        ),
    )[0]
    hidden_win = from_slots(back_hidden)
    up_win = down_conv(padded_g, swapped_up).astype(jnp.bfloat16)
    arrived_up = spread(
        (to_slots(up_win),),
        lambda pieces, offset: jax.tree.map(
            lambda part, own: part.astype(own.dtype),
            shifted(as_sent(pieces), "bricks", offset),
            pieces,
        ),
    )[0]
    grad_pre = (gather_coarse(assignment, arrived_up) * slope).astype(jnp.bfloat16)
    back_grad = spread(
        (coarse_windows(assignment, grad_pre),),
        lambda pieces, offset: jax.tree.map(
            lambda part, own: part.astype(own.dtype),
            shifted(as_sent(pieces), "bricks", peer_count - offset),
            pieces,
        ),
    )[0]
    grad_win = from_slots(back_grad)
    returned = adjoint_conv(grad_win, w_down)[:, 1:9, 1:9, 1:9]
    grad_features = (
        cotangent[0].astype(jnp.float32) + occupied.astype(jnp.float32) * returned
    ).astype(jnp.bfloat16)
    inverse_count = 1.0 / (peer_count * bricks_here)
    term_down = weight_grad(padded_x, grad_win)
    term_up = jnp.swapaxes(weight_grad(padded_g, hidden_win), 1, 2)
    grad_down, grad_up = reduce_terms((term_down, term_up), peer_count, inverse_count)
    return (grad_features[None], grad_down, grad_up)


def solution(mesh):
    return jax.shard_map(
        body,
        mesh=mesh,
        in_specs=(
            P("rep", "bricks", None, None, None, None),
            P("rep", "bricks", None, None, None, None),
            P("rep", "bricks", None),
            P("rep", "bricks"),
            P("rep", "bricks"),
            P(),
            P(),
            P(),
        ),
        out_specs=(
            P("rep", "bricks", None, None, None, None),
            P(None, "bricks"),
            P(None, "bricks"),
        ),
        check_vma=False,
    )
```

```python
import functools

import jax
import jax.numpy as jnp
from jax import lax
from jax.experimental import pallas as pl
from jax.experimental.pallas import tpu as pltpu
from jax.sharding import PartitionSpec as P

OWNERS = 4


NUMBERS = ("NDHWC", "DHWIO", "NDHWC")


def as_sent(shard):
    return jax.tree.map(lambda a: a.astype(jnp.bfloat16) if a.dtype == jnp.float32 else a, shard)


def shifted(shard, axis, by):
    length = lax.axis_size(axis)
    return lax.ppermute(shard, axis, [(i, (i + by) % length) for i in range(length)])


def pad_brick(values):
    return jnp.pad(values, ((0, 0), (1, 2), (1, 2), (1, 2), (0, 0)))


def down_conv(padded, weight):
    return lax.conv_general_dilated(
        padded,
        weight,
        (2, 2, 2),
        "VALID",
        dimension_numbers=NUMBERS,
        preferred_element_type=jnp.float32,
    )


def adjoint_conv(window, weight):
    turned = jnp.swapaxes(weight[::-1, ::-1, ::-1], 3, 4)
    return lax.conv_general_dilated(
        window,
        turned,
        (1, 1, 1),
        ((2, 2), (2, 2), (2, 2)),
        lhs_dilation=(2, 2, 2),
        dimension_numbers=NUMBERS,
        preferred_element_type=jnp.float32,
    )


def weight_grad(padded, window):
    result = lax.conv_general_dilated(
        padded,
        window,
        (1, 1, 1),
        "VALID",
        rhs_dilation=(2, 2, 2),
        dimension_numbers=("CDHWN", "IDHWO", "NDHWC"),
        preferred_element_type=jnp.float32,
    )
    return jnp.transpose(result, (1, 2, 3, 0, 4)).reshape(27, result.shape[0], result.shape[4])


def corner_offsets(corner):
    return (4 * (corner // 4), 4 * (corner // 2 % 2), 4 * (corner % 2))


def spread(items, mover):
    owner_count = items[0].shape[0]
    moved = [tuple((item[0] for item in items))]
    for offset in range(1, owner_count):
        moved.append(mover(tuple((item[offset] for item in items)), offset))
    return tuple((jnp.stack([entry[number] for entry in moved]) for number in range(len(items))))


def reduce_kernel(
    peers, scale, src, out, got_a, kept, got_b, part, got_c, send_a, recv_a, send_b, recv_b, send_c, recv_c, send_d, recv_d
):
    rep = lax.axis_index("rep")
    me = lax.axis_index("bricks")
    low, high = rep % 2, rep // 2
    near = {"rep": high * 2 + 1 - low}
    far = {"rep": (1 - high) * 2 + low}

    def brick(step):
        return (me + step) % peers

    def remote(source, target, send, recv, device):
        return pltpu.make_async_remote_copy(
            src_ref=source,
            dst_ref=target,
            send_sem=send,
            recv_sem=recv,
            device_id=device,
            device_id_type=pl.DeviceIdType.MESH,
        )

    barrier = pltpu.get_barrier_semaphore()
    for device in [near, far] + [{"bricks": brick(step)} for step in range(1, peers)]:
        pl.semaphore_signal(barrier, inc=1, device_id=device, device_id_type=pl.DeviceIdType.MESH)
    pl.semaphore_wait(barrier, peers + 1)

    halves = [1 - high, high]
    order = list(range(1, peers)) + [0]
    copies_a = [
        [
            remote(
                src.at[1 - low, half, brick(step)],
                got_a.at[half, brick(step)],
                send_a.at[number, step],
                recv_a.at[number, step],
                near,
            )
            for step in range(peers)
        ]
        for number, half in enumerate(halves)
    ]
    copies_b = [
        remote(
            kept.at[brick(step)],
            got_b.at[brick(step)],
            send_b.at[step],
            recv_b.at[step],
            far,
        )
        for step in range(peers)
    ]
    for copies in copies_a:
        for step in order:
            copies[step].start()

    def core_sum(number, step):
        copies_a[number][step].wait_recv()
        half, b = halves[number], brick(step)
        return src[low, half, b].astype(jnp.float32) + got_a[half, b].astype(jnp.float32)

    for step in order:
        kept[brick(step)] = core_sum(0, step).astype(jnp.bfloat16)
        copies_b[step].start()

    copies_c = []
    mine = None
    for step in order:
        total = core_sum(1, step)
        copies_b[step].wait_recv()
        b = brick(step)
        total = total + got_b[b].astype(jnp.float32)
        if step == 0:
            mine = total
        else:
            part[b] = total.astype(jnp.bfloat16)
            copy = remote(
                part.at[b],
                got_c.at[step - 1],
                send_c.at[step - 1],
                recv_c.at[step - 1],
                {"bricks": b},
            )
            copy.start()
            copies_c.append(copy)
    for number, copy in enumerate(copies_c):
        copy.wait_recv()
        mine = mine + got_c[number].astype(jnp.float32)
    out[low, high] = mine * scale

    own = out.at[low, high]
    other = out.at[low, 1 - high]
    copies_d = [
        remote(own, own, send_d.at[0], recv_d.at[0], far),
        remote(own, own, send_d.at[1], recv_d.at[1], near),
        remote(other, other, send_d.at[2], recv_d.at[2], near),
    ]
    copies_d[0].start()
    copies_d[1].start()
    copies_d[0].wait_recv()
    copies_d[2].start()
    copies_d[1].wait_recv()
    copies_d[2].wait_recv()
    for copy in copies_a[0] + copies_a[1] + copies_b + copies_c + copies_d:
        copy.wait_send()


def reduce_terms(terms, peers, scale):
    channels = terms[0].shape[1]
    own_rows = channels // peers
    rows = len(terms) * 27 * own_rows
    quarter = -(-rows // 64) * 16
    blocks = [
        jnp.swapaxes(term.astype(jnp.bfloat16).reshape(27, peers, own_rows, channels), 0, 1)
        for term in terms
    ]
    src = jnp.concatenate(blocks, axis=1).reshape(peers, rows, channels)
    src = jnp.pad(src, ((0, 0), (0, 4 * quarter - rows), (0, 0)))
    src = jnp.swapaxes(src.reshape(peers, 4, quarter, channels), 0, 1)
    src = src.reshape(2, 2, peers, quarter, channels)
    dma = pltpu.SemaphoreType.DMA
    wire = jnp.bfloat16
    out = pl.pallas_call(
        functools.partial(reduce_kernel, peers, scale),
        out_shape=jax.ShapeDtypeStruct((2, 2, quarter, channels), jnp.float32),
        in_specs=[pl.BlockSpec(memory_space=pltpu.VMEM)],
        out_specs=pl.BlockSpec(memory_space=pltpu.VMEM),
        scratch_shapes=[
            pltpu.VMEM((2, peers, quarter, channels), wire),
            pltpu.VMEM((peers, quarter, channels), wire),
            pltpu.VMEM((peers, quarter, channels), wire),
            pltpu.VMEM((peers, quarter, channels), wire),
            pltpu.VMEM((peers - 1, quarter, channels), wire),
            dma((2, peers)),
            dma((2, peers)),
            dma((peers,)),
            dma((peers,)),
            dma((peers - 1,)),
            dma((peers - 1,)),
            dma((3,)),
            dma((3,)),
        ],
        compiler_params=pltpu.CompilerParams(
            collective_id=0, has_side_effects=True, vmem_limit_bytes=32 * 1024 * 1024
        ),
    )(src)
    out = out.reshape(4 * quarter, channels)[:rows].reshape(len(terms), 27, own_rows * channels)
    return tuple(out[number] for number in range(len(terms)))


def body(features, cotangent, occupancy, fine_parent, fine_octant, w_down, w_up, bias):
    peer_count = lax.axis_size("bricks")
    my_index = lax.axis_index("bricks")
    bricks_here = features.shape[1]
    channels = features.shape[-1]
    owner_count = OWNERS
    capacity = (bricks_here + owner_count - 1) // owner_count
    coarse_here = (bricks_here + 7) // 8
    slot_count = owner_count * capacity
    occupied = occupancy[0].reshape(bricks_here, 8, 8, 8, 1).astype(jnp.bfloat16)
    padded_x = pad_brick(features[0] * occupied)
    padded_g = pad_brick(cotangent[0] * occupied)
    parent = fine_parent[0]
    octant = fine_octant[0]
    owner_offset = (parent // coarse_here - my_index) % peer_count
    position = jnp.arange(bricks_here, dtype=jnp.int32)
    earlier = (owner_offset[:, None] == owner_offset[None, :]) & (
        position[None, :] < position[:, None]
    )
    slot_of = owner_offset * capacity + jnp.sum(earlier.astype(jnp.int32), axis=1)
    dispatch = (slot_of[None, :] == jnp.arange(slot_count, dtype=jnp.int32)[:, None]).astype(
        jnp.bfloat16
    )
    labels_fine = (1 + parent % coarse_here * 8 + octant).astype(jnp.bfloat16)
    def to_slots(window):
        sent = jnp.dot(
            dispatch, window.reshape(bricks_here, -1), preferred_element_type=jnp.float32
        )
        return sent.astype(jnp.bfloat16).reshape(owner_count, capacity, 5, 5, 5, channels)

    def to_labelled_slots(window):
        cells = window.reshape(bricks_here, 125, channels)
        label = jnp.broadcast_to(labels_fine[:, None, None], (bricks_here, 1, channels))
        sent = jnp.dot(
            dispatch,
            jnp.concatenate([cells, label], axis=1).reshape(bricks_here, -1),
            preferred_element_type=jnp.float32,
        )
        return sent.astype(jnp.bfloat16).reshape(owner_count, capacity, 126, channels)

    def from_slots(arrived):
        taken = jnp.dot(
            dispatch.T, arrived.reshape(slot_count, -1), preferred_element_type=jnp.float32
        )
        return taken.astype(jnp.bfloat16).reshape(bricks_here, 5, 5, 5, channels)

    def gather_coarse(assignment, arrived):
        windows = jnp.dot(
            assignment, arrived.reshape(slot_count, -1), preferred_element_type=jnp.float32
        )
        windows = windows.reshape(coarse_here, 8, 5, 5, 5, channels)
        summed_field = jnp.zeros((coarse_here, 9, 9, 9, channels), jnp.float32)
        for corner in range(8):
            start_x, start_y, start_z = corner_offsets(corner)
            summed_field = summed_field.at[
                :, start_x : start_x + 5, start_y : start_y + 5, start_z : start_z + 5
            ].add(windows[:, corner])
        return summed_field[:, :8, :8, :8]

    def coarse_windows(assignment, coarse_field):
        padded = jnp.pad(coarse_field, ((0, 0), (0, 1), (0, 1), (0, 1), (0, 0)))
        pieces = []
        for corner in range(8):
            start_x, start_y, start_z = corner_offsets(corner)
            pieces.append(
                padded[:, start_x : start_x + 5, start_y : start_y + 5, start_z : start_z + 5]
            )
        stacked = jnp.stack(pieces, axis=1).reshape(coarse_here * 8, -1)
        sent = jnp.dot(assignment.T, stacked, preferred_element_type=jnp.float32)
        return sent.astype(jnp.bfloat16).reshape(owner_count, capacity, 5, 5, 5, channels)

    swapped_up = jnp.swapaxes(w_up, 3, 4)
    down_win = down_conv(padded_x, w_down).astype(jnp.bfloat16)
    arrived_labelled = spread(
        (to_labelled_slots(down_win),),
        lambda pieces, offset: jax.tree.map(
            lambda part, own: part.astype(own.dtype),
            shifted(as_sent(pieces), "bricks", offset),
            pieces,
        ),
    )[0]
    arrived_down = arrived_labelled[:, :, :125]
    flat_labels = arrived_labelled[:, :, 125, 0].reshape(slot_count).astype(jnp.float32)
    targets = (1 + jnp.arange(coarse_here * 8, dtype=jnp.int32)).astype(jnp.float32)
    assignment = (flat_labels[None, :] == targets[:, None]).astype(jnp.bfloat16)
    pre = gather_coarse(assignment, arrived_down) + bias
    sigmoid_pre = jax.nn.sigmoid(pre)
    hidden = jax.nn.silu(pre).astype(jnp.bfloat16)
    slope = sigmoid_pre * (1.0 + pre * (1.0 - sigmoid_pre))
    back_hidden = spread(
        (coarse_windows(assignment, hidden),),
        lambda pieces, offset: jax.tree.map(
            lambda part, own: part.astype(own.dtype),
            shifted(as_sent(pieces), "bricks", peer_count - offset),
            pieces,
        ),
    )[0]
    hidden_win = from_slots(back_hidden)
    up_win = down_conv(padded_g, swapped_up).astype(jnp.bfloat16)
    arrived_up = spread(
        (to_slots(up_win),),
        lambda pieces, offset: jax.tree.map(
            lambda part, own: part.astype(own.dtype),
            shifted(as_sent(pieces), "bricks", offset),
            pieces,
        ),
    )[0]
    grad_pre = (gather_coarse(assignment, arrived_up) * slope).astype(jnp.bfloat16)
    back_grad = spread(
        (coarse_windows(assignment, grad_pre),),
        lambda pieces, offset: jax.tree.map(
            lambda part, own: part.astype(own.dtype),
            shifted(as_sent(pieces), "bricks", peer_count - offset),
            pieces,
        ),
    )[0]
    grad_win = from_slots(back_grad)
    returned = adjoint_conv(grad_win, w_down)[:, 1:9, 1:9, 1:9]
    grad_features = (
        cotangent[0].astype(jnp.float32) + occupied.astype(jnp.float32) * returned
    ).astype(jnp.bfloat16)
    inverse_count = 1.0 / (peer_count * bricks_here)
    term_down = weight_grad(padded_x, grad_win)
    term_up = jnp.swapaxes(weight_grad(padded_g, hidden_win), 1, 2)
    grad_down, grad_up = reduce_terms((term_down, term_up), peer_count, inverse_count)
    return (grad_features[None], grad_down, grad_up)


def solution(mesh):
    return jax.shard_map(
        body,
        mesh=mesh,
        in_specs=(
            P("rep", "bricks", None, None, None, None),
            P("rep", "bricks", None, None, None, None),
            P("rep", "bricks", None),
            P("rep", "bricks"),
            P("rep", "bricks"),
            P(),
            P(),
            P(),
        ),
        out_specs=(
            P("rep", "bricks", None, None, None, None),
            P(None, "bricks"),
            P(None, "bricks"),
        ),
        check_vma=False,
    )
```
